256 devices in a mesh: seq: 256 (over x, z, y, core).
Axes of the slice: x: 4, y: 4, z: 8, core: 2. Of those that a mesh axis runs over, the one named last changes fastest.
Arguments:
- queries: bfloat16 [65536, 1024], P('seq'), may hold values from -6 to 6
- key_rows: bfloat16 [65536, 1024], P('seq'), may hold values from -6 to 6
- value_rows: bfloat16 [65536, 1024], P('seq'), may hold values from -6 to 6
- out_grad: bfloat16 [65536, 1024], P('seq'), may hold values from -6 to 6
- gloss_blocks: int32 [256, 3], replicated, may hold values from -1 to 511, as said below
- gloss_count: int32 [256], replicated, may hold values from 1 to 3
Outputs:
- attended: bfloat16 [65536, 1024], P('seq')
- query_gradient: bfloat16 [65536, 1024], P('seq')
- key_grad: bfloat16 [65536, 1024], P('seq')
- value_grad: bfloat16 [65536, 1024], P('seq')
The draws below stay inside these ranges and needn't reach their ends.
Inputs may be any that keep to these rules, and one draw needn't show every extreme that they name: `gloss_blocks`: entry j of clip c is -1 or a block of one of the 3 clips before c, that is a block from 2 * (c - 3) to 2 * c - 1; it is -1 exactly where the chosen earlier clip would lie before clip 0. The entries of clip c choose each of the 3 earlier clips exactly 1 times, in an order drawn from the seed.
All inputs are finite; a program needn't handle non-finite values.
Results may differ from the reference program's by a relative error of at most 0.011.
Values may be sent and summed in bfloat16 or wider, within the bound.
No kernel may reach another device: no remote copies, remote signals or barrier semaphores. Data moves between devices by JAX's collectives and lax.ppermute only.
A program may use at most 128 MiB of HBM per device.

```python
import jax
import jax.numpy as jnp
from jax import lax

HEADS = 16
HEAD_DIM = 64
MODEL_WIDTH = 1024
BLOCK_FRAMES = 128
BLOCKS_DEV = 2
GLOSS_BLOCKS = 3
SPAN = 3
CAPACITY = 1
CLIPS = 256
NBLOCKS = 512
FRAMES = 65536


def base_draw(base_key, salt_value):
    return jnp.clip(jax.random.normal(jax.random.fold_in(base_key, salt_value), (FRAMES, MODEL_WIDTH), jnp.float32), -6.0, 6.0)


def draw_queries(key, part):
    drawn = base_draw(key, 1)
    return drawn.astype(jnp.bfloat16)


def draw_key_rows(key, part):
    drawn = base_draw(key, 2)
    return drawn.astype(jnp.bfloat16)


def draw_gloss_blocks(key, part):
    order_key, block_key = jax.random.split(jax.random.fold_in(key, 3))
    slot_count = SPAN * CAPACITY
    scores = jax.random.randint(order_key, (CLIPS, slot_count), 0, 1 << 20) * slot_count + jnp.arange(slot_count)[None, :]
    chosen = jnp.argsort(scores, axis=1)[:, :GLOSS_BLOCKS]
    distance = 1 + chosen // CAPACITY
    within = jax.random.randint(block_key, (CLIPS, GLOSS_BLOCKS), 0, BLOCKS_DEV)
    owner_clip = jnp.arange(CLIPS)[:, None] - distance
    return jnp.where(owner_clip >= 0, owner_clip * BLOCKS_DEV + within, -1).astype(jnp.int32)


def with_ends(values, key, smallest, top_value):
    longest = values.shape.index(max(values.shape))
    spots = []
    for shift in (0, 1):
        where = [jax.random.randint(jax.random.fold_in(key, axis), (), 0, length) for axis, length in enumerate(values.shape)]
        where[longest] = (where[longest] + shift) % values.shape[longest]
        spots.append(tuple(where))
    return values.at[spots[0]].set(smallest).at[spots[1]].set(top_value)


def level_of(key, dims, cuts, smallest, high):
    factor_of, own = 1.0, jax.random.fold_in(key, 6)
    for axis_at, blocks in cuts:
        heights = jnp.exp(jax.random.uniform(jax.random.fold_in(own, axis_at), (blocks,), jnp.float32, smallest / len(cuts), high / len(cuts)))
        factor_of = factor_of * jnp.repeat(heights, dims[axis_at] // blocks).reshape([-1 if axis == axis_at else 1 for axis in range(len(dims))])
    return factor_of


def bell_draw(stream_key, dims, width, limit, pieces=(), kind=jnp.bfloat16):
    values = jax.random.normal(stream_key, dims, jnp.float32) * width
    if len(pieces) > 0:
        values = level_of(stream_key, dims, pieces, -0.22, 0.18) * values
    return jnp.clip(values, min=-limit, max=limit).astype(kind)


def setup_inputs(seed: int = 0) -> dict:
    splits = jax.random.split(jax.random.key(seed), 7)
    return {
        "queries": draw_queries(jax.random.fold_in(splits[6], 71), 0),
        "key_rows": draw_key_rows(jax.random.fold_in(splits[6], 71), 0),
        "value_rows": bell_draw(splits[2], (FRAMES, MODEL_WIDTH), 1.0, 6.0, ((0, 256),)),
        "out_grad": bell_draw(splits[3], (FRAMES, MODEL_WIDTH), 1.0, 6.0, ((0, 256),)),
        "gloss_blocks": draw_gloss_blocks(jax.random.fold_in(splits[6], 71), 0),
        "gloss_count": with_ends(jax.random.randint(splits[5], (CLIPS,), 1, GLOSS_BLOCKS + 1), jax.random.fold_in(splits[5], 1), 1, GLOSS_BLOCKS).astype(jnp.int32),
    }


def attend_clip(queries, key_rows, value_rows, out_grad, prev_keys, prev_values, prev_ok, gloss_keys, gloss_values, gloss_ok):
    scores_scale_factor = HEAD_DIM ** -0.5
    shape_four = (BLOCKS_DEV, BLOCK_FRAMES, HEADS, HEAD_DIM)
    query_fourfold = queries.reshape(shape_four).astype(jnp.float32)
    key_four = key_rows.reshape(shape_four)
    value_four = value_rows.reshape(shape_four)
    gradient_fourfold = out_grad.reshape(shape_four).astype(jnp.float32)
    band_key_rows = jnp.concatenate([jnp.concatenate([prev_keys.reshape(1, BLOCK_FRAMES, HEADS, HEAD_DIM), key_four[:-1]], 0), key_four], 1).astype(jnp.float32)
    band_value_rows = jnp.concatenate([jnp.concatenate([prev_values.reshape(1, BLOCK_FRAMES, HEADS, HEAD_DIM), value_four[:-1]], 0), value_four], 1).astype(jnp.float32)
    distant_keys = gloss_keys.reshape(GLOSS_BLOCKS * BLOCK_FRAMES, HEADS, HEAD_DIM).astype(jnp.float32)
    distant_values = gloss_values.reshape(GLOSS_BLOCKS * BLOCK_FRAMES, HEADS, HEAD_DIM).astype(jnp.float32)
    position = jnp.arange(BLOCK_FRAMES)
    key_slot = jnp.arange(2 * BLOCK_FRAMES)
    first_ok = (jnp.arange(BLOCKS_DEV) > 0) | prev_ok
    band_mask = jnp.where(key_slot[None, None, :] < BLOCK_FRAMES, first_ok[:, None, None], (key_slot[None, None, :] - BLOCK_FRAMES) <= position[None, :, None])
    gloss_mask = jnp.repeat(gloss_ok, BLOCK_FRAMES)
    band_scores = jnp.einsum("cqhd,ckhd->chqk", query_fourfold, band_key_rows) * scores_scale_factor
    distant_scores = jnp.einsum("vnas,eas->vane", query_fourfold, distant_keys) * scores_scale_factor
    band_scores = jnp.where(band_mask[:, None], band_scores, -jnp.inf)
    distant_scores = jnp.where(gloss_mask, distant_scores, -jnp.inf)
    row_max = jnp.maximum(jnp.max(band_scores, -1), jnp.max(distant_scores, -1))
    band_exp = jnp.exp(band_scores - row_max[..., None])
    far_exp = jnp.exp(distant_scores - row_max[..., None])
    row_total = jnp.sum(band_exp, -1) + jnp.sum(far_exp, -1)
    band_prob = band_exp / row_total[..., None]
    far_prob = far_exp / row_total[..., None]
    band_half_precision = band_prob.astype(jnp.bfloat16).astype(jnp.float32)
    distant_half_precision = far_prob.astype(jnp.bfloat16).astype(jnp.float32)
    combined_sum = jnp.einsum("lizn,lnix->lzix", band_half_precision, band_value_rows) + jnp.einsum("ofea,afk->oefk", distant_half_precision, distant_values)
    attended = combined_sum.astype(jnp.bfloat16).reshape(BLOCKS_DEV * BLOCK_FRAMES, MODEL_WIDTH)
    row_delta = jnp.transpose(jnp.sum(gradient_fourfold * combined_sum, -1), (0, 2, 1))
    band_dprob = jnp.einsum("cqhd,ckhd->chqk", gradient_fourfold, band_value_rows)
    distant_prob_gradient = jnp.einsum("vnas,eas->vane", gradient_fourfold, distant_values)
    band_score_gradient = (band_prob * (band_dprob - row_delta[..., None]) * scores_scale_factor).astype(jnp.bfloat16).astype(jnp.float32)
    distant_score_gradient = (far_prob * (distant_prob_gradient - row_delta[..., None]) * scores_scale_factor).astype(jnp.bfloat16).astype(jnp.float32)
    query_gradient = jnp.einsum("lizn,lnix->lzix", band_score_gradient, band_key_rows) + jnp.einsum("ofea,afk->oefk", distant_score_gradient, distant_keys)
    query_gradient = query_gradient.astype(jnp.bfloat16).reshape(BLOCKS_DEV * BLOCK_FRAMES, MODEL_WIDTH)
    band_key_grad = jnp.einsum("chqk,cqhd->ckhd", band_score_gradient, query_fourfold)
    band_value_grad = jnp.einsum("chqk,cqhd->ckhd", band_half_precision, gradient_fourfold)
    distant_key_gradient = jnp.einsum("jbwt,jwbu->tbu", distant_score_gradient, query_fourfold).reshape(GLOSS_BLOCKS, BLOCK_FRAMES, MODEL_WIDTH)
    distant_value_gradient = jnp.einsum("jbwt,jwbu->tbu", distant_half_precision, gradient_fourfold).reshape(GLOSS_BLOCKS, BLOCK_FRAMES, MODEL_WIDTH)
    tail_zero = jnp.zeros((1, BLOCK_FRAMES, HEADS, HEAD_DIM), jnp.float32)
    own_key = (band_key_grad[:, BLOCK_FRAMES:] + jnp.concatenate([band_key_grad[1:, :BLOCK_FRAMES], tail_zero], 0)).reshape(BLOCKS_DEV, BLOCK_FRAMES, MODEL_WIDTH)
    own_value = (band_value_grad[:, BLOCK_FRAMES:] + jnp.concatenate([band_value_grad[1:, :BLOCK_FRAMES], tail_zero], 0)).reshape(BLOCKS_DEV, BLOCK_FRAMES, MODEL_WIDTH)
    edge_key = band_key_grad[0, :BLOCK_FRAMES].reshape(BLOCK_FRAMES, MODEL_WIDTH)
    edge_value = band_value_grad[0, :BLOCK_FRAMES].reshape(BLOCK_FRAMES, MODEL_WIDTH)
    return attended, query_gradient, own_key, own_value, edge_key, edge_value, distant_key_gradient, distant_value_gradient


def reference(queries, key_rows, value_rows, out_grad, gloss_blocks, gloss_count):
    clip_frames = BLOCKS_DEV * BLOCK_FRAMES
    query_clips = queries.reshape(CLIPS, clip_frames, MODEL_WIDTH)
    key_clips = key_rows.reshape(CLIPS, clip_frames, MODEL_WIDTH)
    value_clips = value_rows.reshape(CLIPS, clip_frames, MODEL_WIDTH)
    grad_clips = out_grad.reshape(CLIPS, clip_frames, MODEL_WIDTH)
    key_blocks = key_rows.reshape(NBLOCKS, BLOCK_FRAMES, MODEL_WIDTH)
    value_blocks = value_rows.reshape(NBLOCKS, BLOCK_FRAMES, MODEL_WIDTH)

    def one_clip(carry, clip_index):
        key_sum, value_sum = carry
        prev_index = jnp.maximum(clip_index * BLOCKS_DEV - 1, 0).astype(jnp.int32)
        prev_keys = lax.dynamic_index_in_dim(key_blocks, prev_index, 0, keepdims=False)
        prev_values = lax.dynamic_index_in_dim(value_blocks, prev_index, 0, keepdims=False)
        entries = lax.dynamic_index_in_dim(gloss_blocks, clip_index, 0, keepdims=False)
        count_here = lax.dynamic_index_in_dim(gloss_count, clip_index, 0, keepdims=False)
        gloss_ok = (jnp.arange(GLOSS_BLOCKS) < count_here) & (entries >= 0)
        safe_entries = jnp.maximum(entries, 0).astype(jnp.int32)
        gloss_keys = jnp.take(key_blocks, safe_entries, axis=0)
        gloss_values = jnp.take(value_blocks, safe_entries, axis=0)
        results = attend_clip(
            lax.dynamic_index_in_dim(query_clips, clip_index, 0, keepdims=False),
            lax.dynamic_index_in_dim(key_clips, clip_index, 0, keepdims=False),
            lax.dynamic_index_in_dim(value_clips, clip_index, 0, keepdims=False),
            lax.dynamic_index_in_dim(grad_clips, clip_index, 0, keepdims=False),
            prev_keys, prev_values, clip_index > 0, gloss_keys, gloss_values, gloss_ok)
        attended, query_gradient, own_key, own_value, edge_key, edge_value, far_key, far_value = results
        own_index = (clip_index * BLOCKS_DEV + jnp.arange(BLOCKS_DEV)).astype(jnp.int32)
        key_sum = key_sum.at[own_index].add(own_key).at[prev_index].add(edge_key).at[safe_entries].add(far_key)
        value_sum = value_sum.at[own_index].add(own_value).at[prev_index].add(edge_value).at[safe_entries].add(far_value)
        return (key_sum, value_sum), (attended, query_gradient)

    zero_sum = jnp.zeros((NBLOCKS, BLOCK_FRAMES, MODEL_WIDTH), jnp.float32)
    (key_sum, value_sum), (attended, query_gradient) = lax.scan(one_clip, (zero_sum, zero_sum), jnp.arange(CLIPS, dtype=jnp.int32))
    return (attended.reshape(FRAMES, MODEL_WIDTH), query_gradient.reshape(FRAMES, MODEL_WIDTH),
            key_sum.astype(jnp.bfloat16).reshape(FRAMES, MODEL_WIDTH), value_sum.astype(jnp.bfloat16).reshape(FRAMES, MODEL_WIDTH))
```

```python
import jax
import jax.numpy as jnp
from jax import lax
from jax.experimental import pallas as pl
from jax.experimental.pallas import tpu as pltpu
from jax.sharding import PartitionSpec as P

HEAD_DIM = 64
BLOCK = 128
CLIP = 2 * BLOCK
GLOSS = 3
HALF = 512
LANES = 128
Y, Z, X = 4, 8, 4
SCALE = HEAD_DIM**-0.5
NT = (((1,), (1,)), ((), ()))
VMEM_LIMIT = 48 * 1024 * 1024


def place(device):
    chip = device // 2
    return chip // (Y * Z), (chip // Y) % Z, chip % Y, device % 2


def device_at(x, z, y, core):
    return (((x % X) * Z + z % Z) * Y + y % Y) * 2 + core


def send(value, route):
    devices = lax.axis_size("seq")
    pairs = [(i, route(i)) for i in range(devices)]
    return lax.ppermute(value, "seq", [(a, b) for a, b in pairs if b is not None and 0 <= b < devices])


def swap(value):
    return send(value, lambda i: i ^ 1)


def chip_step(value, step):
    return send(value, lambda i: i + 2 * step)


def cross_step(value, step):
    return send(value, lambda i: (i ^ 1) + 2 * step)


def y_step(value, step):
    def route(i):
        x, z, y, core = place(i)
        return device_at(x, z, y + step, core)

    return send(value, route)


def two_chips_on(value):
    pairs = {}
    for i in range(lax.axis_size("seq")):
        x, z, y, core = place(i)
        pairs[device_at(x, z, y - 1, core)] = i + 4
    return send(value, lambda i: pairs[i])


def two_chips_back(value, core_sent):
    pairs = {}
    for i in range(core_sent, lax.axis_size("seq"), 2):
        x, z, y, core = place(i)
        pairs[device_at(x, z, y + 1, core)] = i - core - 3
    return send(value, lambda i: pairs.get(i))


def pack_kernel(head, first, second, own, other):
    h = head[0]
    for n, src in enumerate((first, second)):
        left, right = src[:, :HALF], src[:, HALF:]
        own[n] = jnp.where(h == 0, left, right)
        other[n] = jnp.where(h == 0, right, left)


def pack(head, first, second):
    part = jax.ShapeDtypeStruct((2, CLIP, HALF), jnp.bfloat16)
    rows = pl.BlockSpec((BLOCK, 2 * HALF), lambda r: (r, 0))
    return pl.pallas_call(
        pack_kernel,
        grid=(CLIP // BLOCK,),
        out_shape=(part, part),
        in_specs=[pl.BlockSpec(memory_space=pltpu.SMEM), rows, rows],
        out_specs=(pl.BlockSpec((2, BLOCK, HALF), lambda r: (0, r, 0)),) * 2,
        name="pack",
    )(head, first, second)


def attend_kernel(
    meta,
    own_kv,
    swap_kv,
    own_qg,
    swap_qg,
    same_kv,
    cross_kv,
    far_kv,
    out_mine,
    out_theirs,
    grad_mine,
    grad_theirs,
    grad_same,
    grad_cross,
    grad_far,
    ks,
    vs,
    kts,
    vts,
    qs,
    gs,
    dks,
    dvs,
    outs,
    dqs,
):
    h = meta[0]
    for kv, first in ((own_kv, 5 + 2 * h), (swap_kv, 7 - 2 * h), (same_kv, 1 + 2 * h), (cross_kv, 3 - 2 * h), (far_kv, 0)):
        for r in range(kv.shape[1] // BLOCK):
            kb = kv[0, r * BLOCK : (r + 1) * BLOCK, :]
            vb = kv[1, r * BLOCK : (r + 1) * BLOCK, :]
            ks[first + r] = kb
            vs[first + r] = vb
            kts[first + r] = kb.T
            vts[first + r] = vb.T
    for qg, first in ((own_qg, 2 * h), (swap_qg, 2 - 2 * h)):
        for r in range(2):
            qs[first + r] = qg[0, r * BLOCK : (r + 1) * BLOCK, :]
            gs[first + r] = qg[1, r * BLOCK : (r + 1) * BLOCK, :]
    dks[...] = jnp.zeros_like(dks)
    dvs[...] = jnp.zeros_like(dvs)
    left = lax.broadcasted_iota(jnp.int32, (BLOCK, LANES), 1) < HEAD_DIM
    key_at = lax.broadcasted_iota(jnp.int32, (BLOCK, 2 * BLOCK), 0)
    query_at = lax.broadcasted_iota(jnp.int32, (BLOCK, 2 * BLOCK), 1) % BLOCK
    causal = key_at <= query_at

    def by_head(x):
        zero = jnp.zeros_like(x)
        return jnp.concatenate([jnp.where(left, x, zero), jnp.where(left, zero, x)], 0)

    def of_head(x):
        return jnp.concatenate([x[:HEAD_DIM, :BLOCK], x[HEAD_DIM:, BLOCK:]], 0).T

    for b in range(4):
        clip = b // 2
        index = [5 + b, 4 + b] + [meta[1 + 6 * clip + j] for j in range(GLOSS)]
        keep = [None, (meta[13] > 0) if b == 0 else None] + [meta[4 + 6 * clip + j] > 0 for j in range(GLOSS)]
        qm = by_head(qs[b] * SCALE)
        gm = by_head(gs[b])
        ksel = jnp.concatenate([ks[i] for i in index], 0)
        vsel = jnp.concatenate([vs[i] for i in index], 0)
        scores = lax.dot_general(ksel, qm, NT, preferred_element_type=jnp.float32)
        parts = []
        for n, ok in enumerate(keep):
            part = scores[n * BLOCK : (n + 1) * BLOCK]
            if n == 0:
                part = jnp.where(causal, part, -jnp.inf)
            elif ok is not None:
                part = jnp.where(ok, part, -jnp.inf)
            parts.append(part)
        scores = jnp.concatenate(parts, 0)
        top = jnp.max(scores, 0, keepdims=True)
        weight = jnp.exp(scores - top)
        dprob = lax.dot_general(vsel, gm, NT, preferred_element_type=jnp.float32)
        inverse = 1.0 / jnp.sum(weight, 0, keepdims=True)
        delta = jnp.sum(weight * dprob, 0, keepdims=True) * inverse
        prob = weight * inverse
        dscore = (prob * (dprob - delta)).astype(jnp.bfloat16)
        prob = prob.astype(jnp.bfloat16)
        dv = jnp.dot(prob, gm, preferred_element_type=jnp.float32)
        dk = jnp.dot(dscore, qm, preferred_element_type=jnp.float32)
        for n, i in enumerate(index):
            dks[i] += dk[n * BLOCK : (n + 1) * BLOCK]
            dvs[i] += dv[n * BLOCK : (n + 1) * BLOCK]
        vt = jnp.concatenate([vts[i] for i in index], 1)
        kt = jnp.concatenate([kts[i] for i in index], 1)
        outs[b] = of_head(jnp.dot(vt, prob, preferred_element_type=jnp.float32)).astype(jnp.bfloat16)
        dqs[b] = (of_head(jnp.dot(kt, dscore, preferred_element_type=jnp.float32)) * SCALE).astype(jnp.bfloat16)

    for dst, first in ((out_mine, 2 * h), (out_theirs, 2 - 2 * h)):
        for r in range(2):
            dst[0, r * BLOCK : (r + 1) * BLOCK, :] = outs[first + r]
            dst[1, r * BLOCK : (r + 1) * BLOCK, :] = dqs[first + r]
    for dst, first in ((grad_mine, 5 + 2 * h), (grad_theirs, 7 - 2 * h), (grad_same, 1 + 2 * h), (grad_cross, 3 - 2 * h), (grad_far, 0)):
        for r in range(dst.shape[1] // BLOCK):
            dst[0, r * BLOCK : (r + 1) * BLOCK, :] = dks[first + r].astype(dst.dtype)
            dst[1, r * BLOCK : (r + 1) * BLOCK, :] = dvs[first + r].astype(dst.dtype)


def attend(meta, own_kv, swap_kv, own_qg, swap_qg, same_kv, cross_kv, far_kv):
    def spec(rows):
        return pl.BlockSpec((2, rows, LANES), lambda p: (0, 0, p))

    def shape(rows, dtype):
        return jax.ShapeDtypeStruct((2, rows, HALF), dtype)

    bf16, f32 = jnp.bfloat16, jnp.float32
    return pl.pallas_call(
        attend_kernel,
        grid=(HALF // LANES,),
        out_shape=(shape(CLIP, bf16), shape(CLIP, bf16), shape(CLIP, f32), shape(CLIP, bf16), shape(CLIP, bf16), shape(CLIP, bf16), shape(BLOCK, bf16)),
        in_specs=[pl.BlockSpec(memory_space=pltpu.SMEM)] + [spec(CLIP)] * 6 + [spec(BLOCK)],
        out_specs=(spec(CLIP),) * 6 + (spec(BLOCK),),
        scratch_shapes=[pltpu.VMEM((9, BLOCK, LANES), bf16)] * 4
        + [pltpu.VMEM((4, BLOCK, LANES), bf16)] * 2
        + [pltpu.VMEM((9, BLOCK, LANES), f32)] * 2
        + [pltpu.VMEM((4, BLOCK, LANES), bf16)] * 2,
        compiler_params=pltpu.CompilerParams(vmem_limit_bytes=VMEM_LIMIT),
        name="attend",
    )(meta, own_kv, swap_kv, own_qg, swap_qg, same_kv, cross_kv, far_kv)


def join_kernel(meta, out_mine, out_swap, attended, dq):
    h = meta[0]
    for n, dst in enumerate((attended, dq)):
        dst[:, :HALF] = jnp.where(h == 0, out_mine[n], out_swap[n])
        dst[:, HALF:] = jnp.where(h == 0, out_swap[n], out_mine[n])


def join(meta, out_mine, out_swap):
    whole = jax.ShapeDtypeStruct((CLIP, 2 * HALF), jnp.bfloat16)
    rows = pl.BlockSpec((2, BLOCK, HALF), lambda r: (0, r, 0))
    return pl.pallas_call(
        join_kernel,
        grid=(CLIP // BLOCK,),
        out_shape=(whole, whole),
        in_specs=[pl.BlockSpec(memory_space=pltpu.SMEM), rows, rows],
        out_specs=(pl.BlockSpec((BLOCK, 2 * HALF), lambda r: (r, 0)),) * 2,
        name="join",
    )(meta, out_mine, out_swap)


def total_kernel(meta, mine, swapped, same, cross, far_left, far_right, dk, dv):
    h = meta[0]
    block = pl.program_id(0)
    add_far = jnp.where((h == 1) & (block == meta[14]), 1.0, 0.0).astype(jnp.float32)
    for n, dst in enumerate((dk, dv)):
        own = mine[n] + same[n].astype(jnp.float32)
        other = swapped[n].astype(jnp.float32) + cross[n].astype(jnp.float32)
        first = jnp.where(h == 0, own, other) + far_left[n].astype(jnp.float32) * add_far
        second = jnp.where(h == 0, other, own) + far_right[n].astype(jnp.float32) * add_far
        dst[:, :HALF] = first.astype(jnp.bfloat16)
        dst[:, HALF:] = second.astype(jnp.bfloat16)


def total(meta, mine, swapped, same, cross, far_left, far_right):
    rows = pl.BlockSpec((2, BLOCK, HALF), lambda r: (0, r, 0))
    once = pl.BlockSpec((2, BLOCK, HALF), lambda r: (0, 0, 0))
    whole = jax.ShapeDtypeStruct((CLIP, 2 * HALF), jnp.bfloat16)
    return pl.pallas_call(
        total_kernel,
        grid=(2,),
        out_shape=(whole, whole),
        in_specs=[pl.BlockSpec(memory_space=pltpu.SMEM)] + [rows] * 4 + [once] * 2,
        out_specs=(pl.BlockSpec((BLOCK, 2 * HALF), lambda r: (r, 0)),) * 2,
        name="total",
    )(meta, mine, swapped, same, cross, far_left, far_right)


def plan(gloss_blocks, gloss_count):
    device = lax.axis_index("seq")
    chip = device // 2
    entries = lax.dynamic_slice(gloss_blocks, (2 * chip, 0), (2, GLOSS))
    counts = lax.dynamic_slice(gloss_count, (2 * chip,), (2,))
    index = jnp.maximum(entries - 4 * chip + 5, 0)
    keep = ((entries >= 0) & (jnp.arange(GLOSS)[None, :] < counts[:, None])).astype(jnp.int32)
    later = jnp.minimum(2 * chip + 4, gloss_blocks.shape[0] - 1)
    wanted = lax.dynamic_slice(gloss_blocks, (later, 0), (1, GLOSS))[0]
    far = jnp.sum(jnp.where(wanted == 4 * chip + 3, 1, 0))
    lists = jnp.concatenate([index, keep], 1).reshape(-1)
    head = (device % 2).astype(jnp.int32)
    meta = jnp.concatenate([head[None], lists, (chip > 0).astype(jnp.int32)[None], far.astype(jnp.int32)[None]])
    return meta, far


def shards(queries, key_rows, value_rows, out_grad, gloss_blocks, gloss_count):
    meta, far = plan(gloss_blocks, gloss_count)
    head = (lax.axis_index("seq") % 2).astype(jnp.int32)[None]
    own_kv, other_kv = pack(head, key_rows, value_rows)
    swap_kv = swap(other_kv)
    same_kv = chip_step(own_kv, 1)
    cross_kv = cross_step(other_kv, 1)
    own_qg, other_qg = pack(head, queries, out_grad)
    swap_qg = swap(other_qg)
    odd_kv = jnp.where(head[0] == 1, own_kv, swap_kv)
    far_kv = lax.dynamic_slice(odd_kv, (0, far * BLOCK, 0), (2, BLOCK, HALF))
    far_kv = two_chips_on(y_step(far_kv, -1))
    out_mine, out_theirs, grad_mine, grad_theirs, grad_same, grad_cross, grad_far = attend(
        meta, own_kv, swap_kv, own_qg, swap_qg, same_kv, cross_kv, far_kv
    )
    came_same = chip_step(grad_same, -1)
    came_cross = cross_step(grad_cross, -1)
    leg = y_step(grad_far, 1)
    out_swap = swap(out_theirs)
    grad_swap = swap(grad_theirs)
    far_left = two_chips_back(leg, 0)
    far_right = two_chips_back(leg, 1)
    attended, query_gradient = join(meta, out_mine, out_swap)
    key_grad, value_grad = total(meta, grad_mine, grad_swap, came_same, came_cross, far_left, far_right)
    return attended, query_gradient, key_grad, value_grad


def solution(mesh):
    in_specs = (P("seq", None), P("seq", None), P("seq", None), P("seq", None), P(), P())
    out_specs = (P("seq", None), P("seq", None), P("seq", None), P("seq", None))
    return jax.shard_map(shards, mesh=mesh, in_specs=in_specs, out_specs=out_specs, check_vma=False)
```
